512 devices in a mesh: slab: 64 (over x, y, core), cross: 8 (over z).
Axes of the slice: x: 4, y: 8, z: 8, core: 2. Of those that a mesh axis runs over, the one named last changes fastest.
Arguments:
- positions: int32 [3, 8388608], P(None, ('slab', 'cross')), may hold values from 0 to 2047, as said below
- velocities: float32 [3, 8388608], P(None, ('slab', 'cross')), may hold values from -6 to 6
- counts: int32 [512], P(('slab', 'cross')), may hold values from 1025 to 16384, as said below
- grid_shift: int32 [3], replicated, may hold values from -4 to 3
- axis_index: int32 [256, 256, 128], P('slab', 'cross'), may hold values from 0 to 5
- droplet: int32 [256, 256, 128], P('slab', 'cross'), may hold values 0 or 1
Outputs:
- new_velocities: float32 [3, 8388608], P(None, ('slab', 'cross'))
The draws below stay inside these ranges and needn't reach their ends.
Inputs may be any that keep to these rules, and one draw needn't show every extreme that they name: `counts`: live particles of a device are in its first slots; one device has 16384 live particles and one has 1025. `positions`: the particles in the slots of device (i, j) of the slab and cross axes lie within half a cell of its block: x within [i * 4 * 8 - 8 // 2, (i + 1) * 4 * 8 + 8 // 2) and y likewise with j and 32, taken periodically; components lie in [0, 2048), [0, 2048), [0, 1024).
All inputs are finite; a program needn't handle non-finite values. No bound on the sum of `droplet` on one device may be relied on, other than what follows from the above.
Results may differ from the reference program's by a relative error of at most 0.00002.
Values sent between devices are 32-bit elements; how exact they have to be, the bound alone decides.
A program may use at most 64 MiB of HBM per device.

```python
import math
import jax
import jax.numpy as jnp

CXD = 4
CYD = 32
NZ = 128
PCAP = 16384
QUANT = 8
NFILL = 8
NX = 256
NY = 256
NP = 8388608


def draw_positions(key, part):
    key = jax.random.fold_in(key, 11)
    keys = jax.random.split(key, 3)
    slot_index = jnp.arange(NP, dtype=jnp.int32)
    holder = slot_index // PCAP
    columns = NY // CYD
    slab_place = holder // columns
    column_place = holder - slab_place * columns
    along_x = slab_place * CXD * QUANT - QUANT // 2 + jax.random.randint(keys[0], (NP,), 0, (CXD + 1) * QUANT, dtype=jnp.int32)
    along_y = column_place * CYD * QUANT - QUANT // 2 + jax.random.randint(keys[1], (NP,), 0, (CYD + 1) * QUANT, dtype=jnp.int32)
    along_z = jax.random.randint(keys[2], (NP,), 0, NZ * QUANT, dtype=jnp.int32)
    return jnp.stack([along_x % (NX * QUANT), along_y % (NY * QUANT), along_z]).astype(jnp.int32)


def draw_counts(key, part):
    key = jax.random.fold_in(key, 12)
    keys = jax.random.split(key, 4)
    devices_all = NP // PCAP
    level = jax.random.randint(keys[0], (devices_all,), 0, 4, dtype=jnp.int32)
    jitter = jax.random.randint(keys[1], (devices_all,), 0, PCAP // 16, dtype=jnp.int32)
    loads = PCAP // jnp.left_shift(1, level) - jitter
    fullest = jax.random.randint(keys[2], (), 0, devices_all, dtype=jnp.int32)
    lightest = (fullest + 1 + jax.random.randint(keys[3], (), 0, devices_all - 1, dtype=jnp.int32)) % devices_all
    places = jnp.arange(devices_all, dtype=jnp.int32)
    loads = jnp.where(places == fullest, PCAP, jnp.where(places == lightest, PCAP // 16 + 1, loads))
    return loads.astype(jnp.int32)


def place_ends(array, key, low, top_value):
    place = [jax.random.randint(jax.random.fold_in(key, axis), (), 0, length) for axis, length in enumerate(array.shape)]
    widest = array.shape.index(max(array.shape))
    neighbour = place[:widest] + [(place[widest] + 1) % array.shape[widest]] + place[widest + 1:]
    return array.at[tuple(place)].set(low).at[tuple(neighbour)].set(top_value)


def steps_of(stream_key, shape, shards, smallest, high):
    level, own = 1.0, jax.random.fold_in(stream_key, 6)
    for position, blocks in shards:
        heights = jnp.exp(jax.random.uniform(jax.random.fold_in(own, position), (blocks,), jnp.float32, smallest / len(shards), high / len(shards)))
        level = level * jnp.repeat(heights, shape[position] // blocks).reshape([-1 if axis == position else 1 for axis in range(len(shape))])
    return level


def gaussian(own_key, shape, width, limit, shards=(), held_as=jnp.bfloat16):
    array = jax.random.normal(own_key, shape, jnp.float32) * width
    if len(shards) > 0:
        array = steps_of(own_key, shape, shards, -0.22, 0.18) * array
    return jnp.clip(array, min=-limit, max=limit).astype(held_as)


def setup_inputs(seed: int = 0) -> dict:
    streams_of = jax.random.split(jax.random.key(seed), 7)
    positions = draw_positions(jax.random.fold_in(streams_of[6], 71), 0)
    velocities = gaussian(streams_of[1], (3, NP), 1.0, 6.0, ((1, 512),), jnp.float32)
    counts = draw_counts(jax.random.fold_in(streams_of[6], 71), 0)
    grid_shift = jax.random.randint(streams_of[3], (3,), -(QUANT // 2), QUANT // 2).astype(jnp.int32)
    axis_index = place_ends(jax.random.randint(streams_of[4], (NX, NY, NZ), 0, 6), jax.random.fold_in(streams_of[4], 1), 0, 5).astype(jnp.int32)
    droplet = place_ends((jax.random.randint(streams_of[5], (NX, NY, NZ), 0, 8) < 1).astype(jnp.int32), jax.random.fold_in(streams_of[5], 1), 0, 1)
    return {"positions": positions, "velocities": velocities, "counts": counts, "grid_shift": grid_shift, "axis_index": axis_index, "droplet": droplet}


ANGLE = 130.0 * math.pi / 180.0


def collide(velocity, cell_mean, axis_code):
    relative = velocity - cell_mean
    axis_along = axis_code // 2
    handed = 1.0 - 2.0 * (axis_code % 2).astype(jnp.float32)
    zeros_row = jnp.zeros_like(relative[0])
    cross_first = jnp.where(axis_along == 1, handed * relative[2], jnp.where(axis_along == 2, -handed * relative[1], zeros_row))
    cross_second = jnp.where(axis_along == 0, -handed * relative[2], jnp.where(axis_along == 2, handed * relative[0], zeros_row))
    cross_third = jnp.where(axis_along == 0, handed * relative[1], jnp.where(axis_along == 1, -handed * relative[0], zeros_row))
    crossed = jnp.stack([cross_first, cross_second, cross_third])
    parallel = jnp.stack([axis_along == 0, axis_along == 1, axis_along == 2])
    rotated = jnp.where(parallel, relative, math.cos(ANGLE) * relative + math.sin(ANGLE) * crossed)
    return cell_mean + rotated


def reference(positions, velocities, counts, grid_shift, axis_index, droplet):
    capacity = positions.shape[1]
    slot_index = jnp.arange(capacity, dtype=jnp.int32)
    holder = slot_index // PCAP
    living = (slot_index - holder * PCAP) < counts[holder]
    first_cell = ((positions[0] + grid_shift[0]) // QUANT) % NX
    second_cell = ((positions[1] + grid_shift[1]) // QUANT) % NY
    third_cell = ((positions[2] + grid_shift[2]) // QUANT) % NZ
    flat_cell = ((first_cell * NY + second_cell) * NZ + third_cell).astype(jnp.int32)
    weight = jnp.where(living, 1.0, 0.0).astype(jnp.float32)
    cell_count = NX * NY * NZ
    number = jax.ops.segment_sum(weight, flat_cell, num_segments=cell_count)
    momentum = jnp.stack([jax.ops.segment_sum(velocities[k] * weight, flat_cell, num_segments=cell_count) for k in range(3)])
    fill_level = jnp.where(droplet.reshape(-1) == 1, float(NFILL), 1.0).astype(jnp.float32)
    cell_mean = momentum / jnp.maximum(number, fill_level)
    collided = collide(velocities, jnp.take(cell_mean, flat_cell, axis=1), jnp.take(axis_index.reshape(-1), flat_cell))
    return jnp.where(living, collided, 0.0).astype(jnp.float32)
```

```python
import functools
import math

import jax
import jax.numpy as jnp
from jax import lax
from jax.experimental import pallas as pl
from jax.experimental.pallas import tpu as pltpu
from jax.sharding import PartitionSpec as P

QUANT = 8
NFILL = 8
ANGLE = 130.0 * math.pi / 180.0

F32 = jnp.float32
BF16 = jnp.bfloat16
I32 = jnp.int32
MESH = pl.DeviceIdType.MESH

CX, CY, NZ = 4, 32, 128
HY = CY + 2
ROWS = 104
PITCH = 112
COLS = 2 * NZ
FACE = 40
NONE = PITCH - 1

STEPS = ((-1, 0), (1, 0), (0, -1), (0, 1), (-1, -1), (-1, 1), (1, -1), (1, 1))
BACK = {step: index for index, step in enumerate(STEPS)}


def split(value):
    high = value.astype(BF16)
    low = (value - high.astype(F32)).astype(BF16)
    return high, low


def kernel(
    block,
    counts, shift, pos, vel, axis, drop, out,
    acc, sums, table, code_tab, drop_tab,
    flag_x_low, flag_x_high, flag_y_low, flag_y_high,
    flag_x_got, flag_y_got, flag_d_got,
    sum_y_low, sum_y_high, sum_x_got, sum_y_got, sum_d_got,
    send_sem, recv_sem,
):
    slots = pos.shape[1]
    slabs, crosses = lax.axis_size("slab"), lax.axis_size("cross")
    me_slab, me_cross = lax.axis_index("slab"), lax.axis_index("cross")

    def place(step):
        return (
            lax.rem(me_slab + step[0] + slabs, slabs),
            lax.rem(me_cross + step[1] + crosses, crosses),
        )

    barrier = pltpu.get_barrier_semaphore()
    for step in STEPS:
        pl.semaphore_signal(barrier, inc=1, device_id=place(step), device_id_type=MESH)

    def remote(index, source, target, step):
        return pltpu.make_async_remote_copy(
            src_ref=source,
            dst_ref=target,
            send_sem=send_sem.at[index],
            recv_sem=recv_sem.at[index],
            device_id=place(step),
            device_id_type=MESH,
        )

    anchor_x = me_slab * (CX * QUANT)
    anchor_y = me_cross * (CY * QUANT)
    period_x = slabs * CX * QUANT
    period_y = crosses * CY * QUANT
    count = counts[0]
    shift_x, shift_y, shift_z = shift[0], shift[1], shift[2]

    def cells(base, lanes):
        place_x = pos[0:1, lanes] - anchor_x + QUANT
        place_y = pos[1:2, lanes] - anchor_y + QUANT
        x = ((place_x & (period_x - 1)) + shift_x) >> 3
        y = ((place_y & (period_y - 1)) + shift_y) >> 3
        z = ((pos[2:3, lanes] + shift_z) >> 3) & (NZ - 1)
        living = lax.broadcasted_iota(I32, (1, block), 1) + base < count
        row = jnp.where(living, (x >> 1) * HY + y, NONE)
        column = (x & 1) * NZ + z
        return row, column, living

    def as_bf16(value):
        return value.astype(F32).astype(BF16)

    def column_onehot(ids, column):
        return jnp.where(ids == as_bf16(column), jnp.ones((), BF16), jnp.zeros((), BF16))

    flag_x_low[0] = axis[0]
    flag_x_low[1] = drop[0]
    flag_x_high[0] = axis[CX - 1]
    flag_x_high[1] = drop[CX - 1]
    for plane in range(CX):
        flag_y_low[plane : plane + 1, :] = axis[plane, 0:1, :]
        flag_y_low[CX + plane : CX + plane + 1, :] = drop[plane, 0:1, :]
        flag_y_high[plane : plane + 1, :] = axis[plane, CY - 1 : CY, :]
        flag_y_high[CX + plane : CX + plane + 1, :] = drop[plane, CY - 1 : CY, :]

    acc[...] = jnp.zeros_like(acc)

    def deposit(index, carry):
        base = pl.multiple_of(index * block, block)
        lanes = pl.ds(base, block)
        row, column, _ = cells(base, lanes)
        high, low = split(vel[:, lanes])
        ids = as_bf16(lax.broadcasted_iota(I32, (COLS, block), 0))
        onehot = column_onehot(ids, column)
        here = ids[:PITCH] == as_bf16(row)
        nought = jnp.zeros((), BF16)
        parts = [jnp.where(here, jnp.ones((1, block), BF16), nought)]
        for k in range(3):
            for term in (high, low):
                parts.append(jnp.where(here, term[k : k + 1], nought))
        acc[...] += lax.dot_general(
            jnp.concatenate(parts, axis=0), onehot, (((1,), (1,)), ((), ())),
            preferred_element_type=F32,
        )
        return carry

    half = slots // block // 2
    lax.fori_loop(0, half, deposit, 0)

    pl.semaphore_wait(barrier, len(STEPS))
    flag_copies = []
    for index, step in enumerate(STEPS):
        if step[1] == 0:
            source = flag_x_low if step[0] < 0 else flag_x_high
            target = flag_x_got.at[index]
        else:
            source = flag_y_low if step[1] < 0 else flag_y_high
            target = flag_y_got.at[index - 2] if step[0] == 0 else flag_d_got.at[index - 4]
        copy = remote(index, source, target, step)
        copy.start()
        flag_copies.append(copy)

    lax.fori_loop(half, slots // block, deposit, 0)

    sums[0] = acc[0:ROWS, :]
    for k in range(3):
        first = (1 + 2 * k) * PITCH
        second = first + PITCH
        sums[1 + k] = acc[first : first + ROWS, :] + acc[second : second + ROWS, :]
    for pair in range(3):
        for channel in range(4):
            into = slice(2 * channel, 2 * channel + 2)
            sum_y_low[pair, into, :] = sums[channel, pair * HY : pair * HY + 2, :]
            sum_y_high[pair, into, :] = sums[channel, pair * HY + CY : pair * HY + CY + 2, :]

    sum_copies = []
    for index, step in enumerate(STEPS):
        if step[1] == 0:
            source = sums.at[:, 0:FACE, :] if step[0] < 0 else sums.at[:, ROWS - FACE : ROWS, :]
            target = sum_x_got.at[index]
        else:
            source = sum_y_low if step[1] < 0 else sum_y_high
            target = sum_y_got.at[index - 2]
            if step[0] != 0:
                source = source.at[0 if step[0] < 0 else 2]
                target = sum_d_got.at[index - 4]
        copy = remote(8 + index, source, target, step)
        copy.start()
        sum_copies.append(copy)

    code_tab[...] = jnp.zeros_like(code_tab)
    drop_tab[...] = jnp.zeros_like(drop_tab)
    for copy in flag_copies:
        copy.wait_recv()
    for plane in range(CX + 2):
        pair = plane // 2
        tile = slice(plane % 2 * NZ, plane % 2 * NZ + NZ)
        rows = slice(pair * HY + 1, pair * HY + 1 + CY)
        if plane == 0:
            side, edge = -1, CX - 1
            code_in = flag_x_got[BACK[(1, 0)], 0]
            drop_in = flag_x_got[BACK[(1, 0)], 1]
        elif plane == CX + 1:
            side, edge = 1, 0
            code_in = flag_x_got[BACK[(-1, 0)], 0]
            drop_in = flag_x_got[BACK[(-1, 0)], 1]
        else:
            side, edge = 0, plane - 1
            code_in = axis[plane - 1]
            drop_in = drop[plane - 1]
        code_tab[rows, tile] = code_in
        drop_tab[rows, tile] = drop_in
        for end in (-1, 1):
            row = pair * HY + (0 if end < 0 else HY - 1)
            index = BACK[(-side, -end)]
            got = flag_y_got.at[index - 2] if side == 0 else flag_d_got.at[index - 4]
            code_tab[row : row + 1, tile] = got[edge : edge + 1, :]
            drop_tab[row : row + 1, tile] = got[CX + edge : CX + edge + 1, :]

    for copy in sum_copies:
        copy.wait_send()
        copy.wait_recv()

    pad = FACE - HY
    low = slice(0, HY)
    high = slice(2 * HY, 3 * HY)
    off = ROWS - FACE
    for channel in range(4):
        sums[channel, low, :] += sum_x_got[BACK[(1, 0)], channel, 2 * HY - off : 3 * HY - off, :]
        sums[channel, high, :] += sum_x_got[BACK[(-1, 0)], channel, low, :]
        part = slice(2 * channel, 2 * channel + 2)
        for end in (-1, 1):
            for pair in range(3):
                first = pair * HY + (0 if end < 0 else CY)
                total = sum_y_got[BACK[(0, -end)] - 2, pair, part, :]
                if pair == 0:
                    total = total + sum_d_got[BACK[(1, -end)] - 4, part, :]
                if pair == 2:
                    total = total + sum_d_got[BACK[(-1, -end)] - 4, part, :]
                sums[channel, first : first + 2, :] += total

    fill = jnp.where(drop_tab[...] == 1, float(NFILL), 1.0)
    number = jnp.maximum(sums[0], fill)
    blank = jnp.zeros((PITCH - ROWS, COLS), F32)
    table[0:PITCH, :] = jnp.concatenate([code_tab[...].astype(F32), blank], axis=0).astype(BF16)
    for k in range(3):
        terms = split(jnp.concatenate([sums[1 + k] / number, blank], axis=0))
        for t in range(2):
            first = (1 + 2 * k + t) * PITCH
            table[first : first + PITCH, :] = terms[t]

    cosine, sine = math.cos(ANGLE), math.sin(ANGLE)

    def turn(index, carry):
        base = pl.multiple_of(index * block, block)
        lanes = pl.ds(base, block)
        row, column, living = cells(base, lanes)
        onehot = column_onehot(as_bf16(lax.broadcasted_iota(I32, (COLS, block), 0)), column)
        here = lax.broadcasted_iota(I32, (PITCH, block), 0) == row

        def pick(*channels):
            found = None
            for channel in channels:
                rows = table[channel * PITCH : (channel + 1) * PITCH, :]
                term = jnp.dot(rows, onehot, preferred_element_type=F32)
                found = term if found is None else found + term
            return jnp.sum(jnp.where(here, found, 0.0), axis=0, keepdims=True)

        code = pick(0)
        mean = [pick(1 + 2 * k, 2 + 2 * k) for k in range(3)]
        rel = [vel[k : k + 1, lanes] - mean[k] for k in range(3)]
        along_x = code < 1.5
        along_y = (code > 1.5) & (code < 3.5)
        along_z = code > 3.5
        odd = (code == 1.0) | (code == 3.0) | (code == 5.0)
        turn_by = jnp.where(odd, -sine, sine)
        plain = [cosine * r for r in rel]
        cross = [turn_by * r for r in rel]
        new_x = jnp.where(along_x, rel[0], plain[0] + jnp.where(along_y, cross[2], -cross[1]))
        new_y = jnp.where(along_y, rel[1], plain[1] + jnp.where(along_x, -cross[2], cross[0]))
        new_z = jnp.where(along_z, rel[2], plain[2] + jnp.where(along_x, cross[1], -cross[0]))
        for k, new in enumerate((new_x, new_y, new_z)):
            out[k : k + 1, lanes] = jnp.where(living, mean[k] + new, 0.0)
        return carry

    lax.fori_loop(0, slots // block, turn, 0)

    for copy in flag_copies:
        copy.wait_send()


def body(positions, velocities, counts, grid_shift, axis_index, droplet):
    smem = pl.BlockSpec(memory_space=pltpu.SMEM)
    vmem = pl.BlockSpec(memory_space=pltpu.VMEM)
    block = 2048
    return pl.pallas_call(
        functools.partial(kernel, block),
        out_shape=jax.ShapeDtypeStruct(velocities.shape, F32),
        in_specs=[smem, smem, vmem, vmem, vmem, vmem],
        out_specs=vmem,
        scratch_shapes=[
            pltpu.VMEM((7 * PITCH, COLS), F32),
            pltpu.VMEM((4, ROWS, COLS), F32),
            pltpu.VMEM((7 * PITCH, COLS), BF16),
            pltpu.VMEM((ROWS, COLS), I32),
            pltpu.VMEM((ROWS, COLS), I32),
            pltpu.VMEM((2, CY, NZ), I32),
            pltpu.VMEM((2, CY, NZ), I32),
            pltpu.VMEM((2 * CX, NZ), I32),
            pltpu.VMEM((2 * CX, NZ), I32),
            pltpu.VMEM((2, 2, CY, NZ), I32),
            pltpu.VMEM((2, 2 * CX, NZ), I32),
            pltpu.VMEM((4, 2 * CX, NZ), I32),
            pltpu.VMEM((3, 8, COLS), F32),
            pltpu.VMEM((3, 8, COLS), F32),
            pltpu.VMEM((2, 4, FACE, COLS), F32),
            pltpu.VMEM((2, 3, 8, COLS), F32),
            pltpu.VMEM((4, 8, COLS), F32),
            pltpu.SemaphoreType.DMA((16,)),
            pltpu.SemaphoreType.DMA((16,)),
        ],
        compiler_params=pltpu.CompilerParams(
            collective_id=0, has_side_effects=True, vmem_limit_bytes=48 << 20
        ),
        name="collision_step",
    )(counts, grid_shift, positions, velocities, axis_index, droplet)


def solution(mesh):
    placed = (
        P(None, ("slab", "cross")),
        P(None, ("slab", "cross")),
        P(("slab", "cross")),
        P(),
        P("slab", "cross", None),
        P("slab", "cross", None),
    )
    return jax.shard_map(
        body, mesh=mesh, in_specs=placed, out_specs=P(None, ("slab", "cross")), check_vma=False
    )
```

```python
import functools
import math

import jax
import jax.numpy as jnp
from jax import lax
from jax.experimental import pallas as pl
from jax.experimental.pallas import tpu as pltpu
from jax.sharding import PartitionSpec as P

QUANT = 8
NFILL = 8
ANGLE = 130.0 * math.pi / 180.0

F32 = jnp.float32
BF16 = jnp.bfloat16
I32 = jnp.int32
MESH = pl.DeviceIdType.MESH

CX, CY, NZ = 4, 32, 128
COLS = 2 * NZ
OUTER, EDGE, INNER = 64, 16, 32
EDGE_AT = OUTER
INNER_AT = OUTER + EDGE
NONE = 127
FIRST = OUTER + EDGE
HALF = OUTER // 2
MID = CY - 2

STEPS = ((-1, 0), (1, 0), (0, -1), (0, 1), (-1, -1), (-1, 1), (1, -1), (1, 1))
SENT_BY = {step: index for index, step in enumerate(STEPS)}


def split(value):
    high = value.astype(BF16)
    low = (value - high.astype(F32)).astype(BF16)
    return high, low


def as_bf16(value):
    return value.astype(F32).astype(BF16)


def kernel(
    block,
    counts_in, shift_in, pos_in, vel_in, axis_in, drop_in, out,
    counts, shift, pos, vel, axis, drop, load_sem,
    rows, onehots, picked,
    acc_first, acc_inner, sum_outer, sum_inner, sum_edge, part_edge,
    table_outer, table_inner, table_edge,
    code_outer, drop_outer, code_inner, drop_inner, code_edge, drop_edge,
    flag_x_low, flag_x_high, flag_y_low, flag_y_high,
    flag_x_got, flag_y_got, flag_d_got,
    outer_got, edge_x_got, edge_y_got, edge_d_got,
    send_sem, recv_sem,
):
    slots = pos.shape[1]
    slabs, crosses = lax.axis_size("slab"), lax.axis_size("cross")
    me_slab, me_cross = lax.axis_index("slab"), lax.axis_index("cross")

    def place(step):
        return (
            lax.rem(me_slab + step[0] + slabs, slabs),
            lax.rem(me_cross + step[1] + crosses, crosses),
        )

    barrier = pltpu.get_barrier_semaphore()
    for step in STEPS:
        pl.semaphore_signal(barrier, inc=1, device_id=place(step), device_id_type=MESH)

    loads = [
        pltpu.make_async_copy(source, target, load_sem.at[index])
        for index, (source, target) in enumerate((
            (counts_in, counts), (shift_in, shift), (pos_in, pos),
            (vel_in, vel), (axis_in, axis), (drop_in, drop),
        ))
    ]
    for load in loads:
        load.start()

    def remote(index, source, target, step):
        return pltpu.make_async_remote_copy(
            src_ref=source,
            dst_ref=target,
            send_sem=send_sem.at[index],
            recv_sem=recv_sem.at[index],
            device_id=place(step),
            device_id_type=MESH,
        )

    def for_blocks(step):
        if slots == block:
            step(0)
        else:
            def run(index, carry):
                step(pl.multiple_of(index * block, block))
                return carry

            lax.fori_loop(0, slots // block, run, 0)

    acc_first[...] = jnp.zeros_like(acc_first)
    acc_inner[...] = jnp.zeros_like(acc_inner)
    for ref in (code_outer, drop_outer, code_inner, drop_inner, code_edge, drop_edge, sum_edge):
        ref[...] = jnp.zeros_like(ref)

    for load in loads[:4]:
        load.wait()
    anchor_x = me_slab * (CX * QUANT)
    anchor_y = me_cross * (CY * QUANT)
    period_x = slabs * CX * QUANT
    period_y = crosses * CY * QUANT
    count = counts[0]
    shift_x, shift_y, shift_z = shift[0], shift[1], shift[2]

    def find(base):
        lanes = pl.ds(base, block)
        place_x = pos[0:1, lanes] - anchor_x + QUANT
        place_y = pos[1:2, lanes] - anchor_y + QUANT
        x = ((place_x & (period_x - 1)) + shift_x) >> 3
        y = ((place_y & (period_y - 1)) + shift_y) >> 3
        z = ((pos[2:3, lanes] + shift_z) >> 3) & (NZ - 1)
        pair = x >> 1
        first = jnp.where(pair == 1, INNER_AT - 2, pair * (HALF // 2) - 2)
        at_low, at_high = y < 2, y >= CY
        row = jnp.where(at_low | at_high, EDGE_AT + pair * 4 + jnp.where(at_high, -MID, 0), first) + y
        living = lax.broadcasted_iota(I32, (1, block), 1) + base < count
        row = jnp.where(living, row, NONE)
        rows[:, lanes] = row
        column = as_bf16((x & 1) * NZ + z)
        ids = as_bf16(lax.broadcasted_iota(I32, (COLS, block), 0))
        onehot = jnp.where(ids == column, jnp.ones((), BF16), jnp.zeros((), BF16))
        onehots[:, lanes] = onehot
        return row, onehot

    def deposit(acc, first, pitch, base):
        lanes = pl.ds(base, block)
        if first == 0:
            row, onehot = find(base)
        else:
            row, onehot = rows[:, lanes], onehots[:, lanes]
        high, low = split(vel[:, lanes])
        ids = as_bf16(lax.broadcasted_iota(I32, (pitch, block), 0) + first)
        here = ids == as_bf16(row)
        nought = jnp.zeros((), BF16)
        parts = [jnp.where(here, jnp.ones((1, block), BF16), nought)]
        for k in range(3):
            for term in (high, low):
                parts.append(jnp.where(here, term[k : k + 1], nought))
        acc[...] += lax.dot_general(
            jnp.concatenate(parts, axis=0), onehot, (((1,), (1,)), ((), ())),
            preferred_element_type=F32,
        )

    def total(acc, pitch, channel, first, size):
        if channel == 0:
            return acc[first : first + size, :]
        high = (2 * channel - 1) * pitch + first
        low = high + pitch
        return acc[high : high + size, :] + acc[low : low + size, :]

    for_blocks(functools.partial(deposit, acc_first, 0, FIRST))

    for channel in range(4):
        sum_outer[channel] = total(acc_first, FIRST, channel, 0, OUTER)
        edge = total(acc_first, FIRST, channel, EDGE_AT, EDGE)
        for pair in range(3):
            for side in range(2):
                at = side * 8 + channel * 2
                part_edge[pair, at : at + 2, :] = edge[pair * 4 + side * 2 : pair * 4 + side * 2 + 2, :]
    for load in loads[4:]:
        load.wait()
    flag_x_low[0] = axis[0]
    flag_x_low[1] = drop[0]
    flag_x_high[0] = axis[CX - 1]
    flag_x_high[1] = drop[CX - 1]
    for plane in range(CX):
        flag_y_low[plane : plane + 1, :] = axis[plane, 0:1, :]
        flag_y_low[CX + plane : CX + plane + 1, :] = drop[plane, 0:1, :]
        flag_y_high[plane : plane + 1, :] = axis[plane, CY - 1 : CY, :]
        flag_y_high[CX + plane : CX + plane + 1, :] = drop[plane, CY - 1 : CY, :]

    pl.semaphore_wait(barrier, len(STEPS))

    x_copies = []
    for index, step in enumerate(STEPS[:2]):
        half = slice(0, HALF) if step[0] < 0 else slice(HALF, OUTER)
        x_copies.append(remote(16 + index, sum_outer.at[:, half, :], outer_got.at[index], step))
        source = flag_x_low if step[0] < 0 else flag_x_high
        x_copies.append(remote(index, source, flag_x_got.at[index], step))
    edge_copies = []
    for index, step in enumerate(STEPS):
        ends = slice(0, 16) if step[1] == 0 else slice(0, 8) if step[1] < 0 else slice(8, 16)
        if step[0] == 0:
            source, target = part_edge.at[:, ends, :], edge_y_got.at[index - 2]
        else:
            source = part_edge.at[0 if step[0] < 0 else 2, ends, :]
            target = edge_x_got.at[index] if step[1] == 0 else edge_d_got.at[index - 4]
        edge_copies.append(remote(8 + index, source, target, step))
        if step[1] != 0:
            source = flag_y_low if step[1] < 0 else flag_y_high
            target = flag_y_got.at[index - 2] if step[0] == 0 else flag_d_got.at[index - 4]
            edge_copies.append(remote(index, source, target, step))
    for copy in x_copies + edge_copies:
        copy.start()

    def fill_table(table, pitch, sums, code, wall):
        number = jnp.maximum(sums[0], jnp.where(wall[...] == 1, float(NFILL), 1.0))
        for k in range(3):
            high, low = split(sums[1 + k] / number)
            table[k * pitch : (k + 1) * pitch, :] = high
            table[(4 + k) * pitch : (5 + k) * pitch, :] = low
        table[3 * pitch : 4 * pitch, :] = as_bf16(code[...])

    def pick(table, pitch, first, base):
        lanes = pl.ds(base, block)
        onehot = onehots[:, lanes]
        here = lax.broadcasted_iota(I32, (pitch, block), 0) + first == rows[:, lanes]
        highs = jnp.dot(table[0 : 4 * pitch, :], onehot, preferred_element_type=F32)
        lows = jnp.dot(table[4 * pitch : 7 * pitch, :], onehot, preferred_element_type=F32)
        found = []
        for k in range(4):
            part = highs[k * pitch : (k + 1) * pitch]
            if k < 3:
                part = part + lows[k * pitch : (k + 1) * pitch]
            found.append(jnp.sum(jnp.where(here, part, 0.0), axis=0, keepdims=True))
        return found

    for_blocks(functools.partial(deposit, acc_inner, INNER_AT, INNER))
    for channel in range(4):
        sum_inner[channel] = total(acc_inner, INNER, channel, 0, INNER)
    for tile in range(2):
        lanes = slice(tile * NZ, (tile + 1) * NZ)
        code_inner[0:MID, lanes] = axis[1 + tile, 1 : CY - 1, :]
        drop_inner[0:MID, lanes] = drop[1 + tile, 1 : CY - 1, :]
    fill_table(table_inner, INNER, sum_inner, code_inner, drop_inner)

    def pick_inner(base):
        for k, found in enumerate(pick(table_inner, INNER, INNER_AT, base)):
            picked[k : k + 1, pl.ds(base, block)] = found

    for_blocks(pick_inner)

    from_left, from_right = SENT_BY[(1, 0)], SENT_BY[(-1, 0)]
    for copy in x_copies:
        copy.wait_recv()
    for flag, (own, code) in enumerate(((axis, code_outer), (drop, drop_outer))):
        code[0:MID, 0:NZ] = flag_x_got[from_left, flag, 1 : CY - 1, :]
        code[0:MID, NZ:COLS] = own[0, 1 : CY - 1, :]
        code[HALF : HALF + MID, 0:NZ] = own[CX - 1, 1 : CY - 1, :]
        code[HALF : HALF + MID, NZ:COLS] = flag_x_got[from_right, flag, 1 : CY - 1, :]
    both = [
        jnp.concatenate(
            [
                sum_outer[channel, 0:HALF, :] + outer_got[from_left, channel],
                sum_outer[channel, HALF:OUTER, :] + outer_got[from_right, channel],
            ],
            axis=0,
        )
        for channel in range(4)
    ]
    fill_table(table_outer, OUTER, both, code_outer, drop_outer)

    def pick_outer(base):
        for k, found in enumerate(pick(table_outer, OUTER, 0, base)):
            picked[k : k + 1, pl.ds(base, block)] += found

    for_blocks(pick_outer)

    for copy in edge_copies:
        copy.wait_recv()
    for pair in range(3):
        for side, end in enumerate((-1, 1)):
            ends = slice(side * 8, side * 8 + 8)
            whole = part_edge[pair, ends, :] + edge_y_got[SENT_BY[(0, -end)] - 2, pair]
            if pair != 1:
                step = 1 if pair == 0 else -1
                whole = whole + edge_x_got[SENT_BY[(step, 0)], ends, :]
                whole = whole + edge_d_got[SENT_BY[(step, -end)] - 4]
            for channel in range(4):
                at = pair * 4 + side * 2
                sum_edge[channel, at : at + 2, :] = whole[2 * channel : 2 * channel + 2]
            for tile in range(2):
                plane = 2 * pair + tile
                lanes = slice(tile * NZ, (tile + 1) * NZ)
                beyond = -1 if plane == 0 else 1 if plane == CX + 1 else 0
                last = CX - 1 if plane == 0 else 0 if plane == CX + 1 else plane - 1
                inside = 0 if side == 0 else CY - 1
                halo = flag_y_got.at[SENT_BY[(0, -end)] - 2]
                if beyond != 0:
                    halo = flag_d_got.at[SENT_BY[(-beyond, -end)] - 4]
                near = pair * 4 + (1 if side == 0 else 2)
                far = pair * 4 + (0 if side == 0 else 3)
                for flag, (own, code) in enumerate(((axis, code_edge), (drop, drop_edge))):
                    if beyond == 0:
                        value = own[last, inside : inside + 1, :]
                    else:
                        value = flag_x_got[SENT_BY[(-beyond, 0)], flag, inside : inside + 1, :]
                    code[near : near + 1, lanes] = value
                    code[far : far + 1, lanes] = halo[flag * CX + last : flag * CX + last + 1, :]
    fill_table(table_edge, EDGE, sum_edge, code_edge, drop_edge)

    cosine, sine = math.cos(ANGLE), math.sin(ANGLE)

    def finish(base):
        lanes = pl.ds(base, block)
        found = pick(table_edge, EDGE, EDGE_AT, base)
        mean = [picked[k : k + 1, lanes] + found[k] for k in range(3)]
        code = picked[3:4, lanes] + found[3]
        rel = [vel[k : k + 1, lanes] - mean[k] for k in range(3)]
        along_x = code < 1.5
        along_y = (code > 1.5) & (code < 3.5)
        along_z = code > 3.5
        odd = (code == 1.0) | (code == 3.0) | (code == 5.0)
        turn_by = jnp.where(odd, -sine, sine)
        plain = [cosine * r for r in rel]
        cross = [turn_by * r for r in rel]
        new_x = jnp.where(along_x, rel[0], plain[0] + jnp.where(along_y, cross[2], -cross[1]))
        new_y = jnp.where(along_y, rel[1], plain[1] + jnp.where(along_x, -cross[2], cross[0]))
        new_z = jnp.where(along_z, rel[2], plain[2] + jnp.where(along_x, cross[1], -cross[0]))
        living = rows[:, lanes] != NONE
        for k, new in enumerate((new_x, new_y, new_z)):
            out[k : k + 1, lanes] = jnp.where(living, mean[k] + new, 0.0)

    for_blocks(finish)

    for copy in x_copies + edge_copies:
        copy.wait_send()


def body(positions, velocities, counts, grid_shift, axis_index, droplet):
    hbm = pl.BlockSpec(memory_space=pl.ANY)
    slots = positions.shape[1]
    block = BLOCK
    cells = (CX, CY, NZ)
    vmem = pltpu.VMEM
    return pl.pallas_call(
        functools.partial(kernel, block),
        out_shape=jax.ShapeDtypeStruct(velocities.shape, F32),
        in_specs=[hbm] * 6,
        out_specs=pl.BlockSpec(memory_space=pltpu.VMEM),
        scratch_shapes=[
            pltpu.SMEM((1,), I32), pltpu.SMEM((3,), I32),
            vmem((3, slots), I32), vmem((3, slots), F32), vmem(cells, I32), vmem(cells, I32),
            pltpu.SemaphoreType.DMA((6,)),
            vmem((1, slots), I32), vmem((COLS, slots), BF16), vmem((4, slots), F32),
            vmem((7 * FIRST, COLS), F32), vmem((7 * INNER, COLS), F32),
            vmem((4, OUTER, COLS), F32), vmem((4, INNER, COLS), F32), vmem((4, EDGE, COLS), F32),
            vmem((3, 16, COLS), F32),
            vmem((7 * OUTER, COLS), BF16), vmem((7 * INNER, COLS), BF16), vmem((7 * EDGE, COLS), BF16),
            vmem((OUTER, COLS), I32), vmem((OUTER, COLS), I32),
            vmem((INNER, COLS), I32), vmem((INNER, COLS), I32),
            vmem((EDGE, COLS), I32), vmem((EDGE, COLS), I32),
            vmem((2, CY, NZ), I32), vmem((2, CY, NZ), I32),
            vmem((2 * CX, NZ), I32), vmem((2 * CX, NZ), I32),
            vmem((2, 2, CY, NZ), I32), vmem((2, 2 * CX, NZ), I32), vmem((4, 2 * CX, NZ), I32),
            vmem((2, 4, HALF, COLS), F32), vmem((2, 16, COLS), F32),
            vmem((2, 3, 8, COLS), F32), vmem((4, 8, COLS), F32),
            pltpu.SemaphoreType.DMA((18,)),
            pltpu.SemaphoreType.DMA((18,)),
        ],
        compiler_params=pltpu.CompilerParams(
            collective_id=0, has_side_effects=True, vmem_limit_bytes=VMEM_MIB << 20
        ),
        name="collision_step",
    )(counts, grid_shift, positions, velocities, axis_index, droplet)


BLOCK = 8192
VMEM_MIB = 58


def solution(mesh):
    placed = (
        P(None, ("slab", "cross")),
        P(None, ("slab", "cross")),
        P(("slab", "cross")),
        P(),
        P("slab", "cross", None),
        P("slab", "cross", None),
    )
    return jax.shard_map(
        body, mesh=mesh, in_specs=placed, out_specs=P(None, ("slab", "cross")), check_vma=False
    )
```

```python
import functools
import math

import jax
import jax.numpy as jnp
from jax import lax
from jax.experimental import pallas as pl
from jax.experimental.pallas import tpu as pltpu
from jax.sharding import PartitionSpec as P

QUANT = 8
NFILL = 8
ANGLE = 130.0 * math.pi / 180.0

F32 = jnp.float32
BF16 = jnp.bfloat16
I32 = jnp.int32
MESH = pl.DeviceIdType.MESH

CX, CY, NZ = 4, 32, 128
COLS = 2 * NZ
OUTER, EDGE, INNER = 64, 16, 32
EDGE_AT = OUTER
INNER_AT = OUTER + EDGE
FIRST = OUTER + EDGE
NONE = 127
HALF = OUTER // 2
MID = CY - 2

STEPS = ((-1, 0), (1, 0), (0, -1), (0, 1), (-1, -1), (-1, 1), (1, -1), (1, 1))
SENT_BY = {step: index for index, step in enumerate(STEPS)}


def split(value):
    high = value.astype(BF16)
    low = (value - high.astype(F32)).astype(BF16)
    return high, low


def as_bf16(value):
    return value.astype(F32).astype(BF16)


def kernel(
    block,
    counts_in, shift_in, pos_in, vel_in, axis_in, drop_in, out_hbm,
    counts, shift, pos_x, pos_y, pos_z, vel_x, vel_y, vel_z, axis, drop, out_x, out_y, out_z, load_sem,
    rows, onehots, mean_x, mean_y, mean_z, codes,
    acc_first, acc_inner, sum_outer, sum_inner, sum_edge, part_edge,
    table_outer, table_inner, table_edge,
    code_outer, drop_outer, code_inner, drop_inner, code_edge, drop_edge,
    flag_x_low, flag_x_high, flag_y_low, flag_y_high,
    flag_x_got, flag_y_got, flag_d_got,
    outer_got, edge_x_got, edge_y_got, edge_d_got,
    send_sem, recv_sem, late_sem,
):
    slots = rows.shape[1]
    vel = (vel_x, vel_y, vel_z)
    outs = (out_x, out_y, out_z)
    picked = (mean_x, mean_y, mean_z, codes)
    slabs, crosses = lax.axis_size("slab"), lax.axis_size("cross")
    me_slab, me_cross = lax.axis_index("slab"), lax.axis_index("cross")

    def place(step):
        return (
            lax.rem(me_slab + step[0] + slabs, slabs),
            lax.rem(me_cross + step[1] + crosses, crosses),
        )

    first_in = me_cross == 0
    last_in = me_cross == crosses - 1

    def greet(semaphore, ends):
        for step in STEPS:
            if step[1] in ends:
                pl.semaphore_signal(semaphore, inc=1, device_id=place(step), device_id_type=MESH)

    barrier = pltpu.get_barrier_semaphore()
    greet(barrier, (-1, 0))
    pl.when(jnp.logical_not(last_in))(lambda: greet(barrier, (1,)))

    loads = [
        pltpu.make_async_copy(source, target, load_sem.at[index])
        for index, (source, target) in enumerate((
            (counts_in, counts), (shift_in, shift),
            (pos_in.at[0:1, :], pos_x), (pos_in.at[1:2, :], pos_y), (pos_in.at[2:3, :], pos_z),
            (vel_in.at[0:1, :], vel_x), (vel_in.at[1:2, :], vel_y), (vel_in.at[2:3, :], vel_z),
            (axis_in, axis), (drop_in, drop),
        ))
    ]
    for load in loads:
        load.start()

    def remote(index, source, target, step):
        return pltpu.make_async_remote_copy(
            src_ref=source,
            dst_ref=target,
            send_sem=send_sem.at[index],
            recv_sem=recv_sem.at[index],
            device_id=place(step),
            device_id_type=MESH,
        )

    def for_blocks(step, size):
        def run(index, carry):
            step(pl.multiple_of(index * size, size), size)
            return carry

        lax.fori_loop(0, slots // size, run, 0)

    acc_first[...] = jnp.zeros_like(acc_first)
    acc_inner[...] = jnp.zeros_like(acc_inner)
    for ref in (code_outer, drop_outer, code_inner, drop_inner, code_edge, drop_edge, sum_edge):
        ref[...] = jnp.zeros_like(ref)

    anchor_x = me_slab * (CX * QUANT)
    anchor_y = me_cross * (CY * QUANT)
    period_x = slabs * CX * QUANT
    period_y = crosses * CY * QUANT
    for load in loads[:8]:
        load.wait()
    count = counts[0, 0]
    shift_x, shift_y, shift_z = shift[0], shift[1], shift[2]

    def find(base, size):
        lanes = pl.ds(base, size)
        x = (((pos_x[:, lanes] - anchor_x + QUANT) & (period_x - 1)) + shift_x) >> 3
        y = (((pos_y[:, lanes] - anchor_y + QUANT) & (period_y - 1)) + shift_y) >> 3
        z = ((pos_z[:, lanes] + shift_z) >> 3) & (NZ - 1)
        pair = x >> 1
        at_low, at_high = y < 2, y >= CY
        edge = pair * 4 + jnp.where(at_high, EDGE_AT - MID, EDGE_AT)
        other = jnp.where(pair == 1, INNER_AT - 2, pair * (HALF // 2) - 2)
        row = jnp.where(at_low | at_high, edge, other) + y
        living = lax.broadcasted_iota(I32, (1, size), 1) + base < count
        row = jnp.where(living, row, NONE)
        rows[:, lanes] = row
        column = as_bf16((x & 1) * NZ + z)
        ids = as_bf16(lax.broadcasted_iota(I32, (COLS, size), 0))
        onehot = jnp.where(ids == column, jnp.ones((), BF16), jnp.zeros((), BF16))
        onehots[:, lanes] = onehot
        return row, onehot

    def deposit(acc, first, pitch, base, size):
        lanes = pl.ds(base, size)
        if first == 0:
            row, onehot = find(base, size)
        else:
            row, onehot = rows[:, lanes], onehots[:, lanes]
        ids = as_bf16(lax.broadcasted_iota(I32, (pitch, size), 0) + first)
        here = ids == as_bf16(row)
        nought = jnp.zeros((), BF16)
        parts = [jnp.where(here, jnp.ones((1, size), BF16), nought)]
        for k in range(3):
            for term in split(vel[k][:, lanes]):
                parts.append(jnp.where(here, term, nought))
        acc[...] += lax.dot_general(
            jnp.concatenate(parts, axis=0), onehot, (((1,), (1,)), ((), ())),
            preferred_element_type=F32,
        )

    def total(acc, pitch, channel, first, size):
        if channel == 0:
            return acc[first : first + size, :]
        high = (2 * channel - 1) * pitch + first
        low = high + pitch
        return acc[high : high + size, :] + acc[low : low + size, :]

    def fill_table(table, pitch, sums, code, wall):
        number = jnp.maximum(sums[0], jnp.where(wall[...] == 1, float(NFILL), 1.0))
        for k in range(3):
            high, low = split(sums[1 + k] / number)
            table[k * pitch : (k + 1) * pitch, :] = high
            table[(4 + k) * pitch : (5 + k) * pitch, :] = low
        table[3 * pitch : 4 * pitch, :] = as_bf16(code[...])

    def pick(table, pitch, first, base, size):
        lanes = pl.ds(base, size)
        onehot = onehots[:, lanes]
        here = lax.broadcasted_iota(I32, (pitch, size), 0) + first == rows[:, lanes]
        terms = jnp.dot(table[...], onehot, preferred_element_type=F32)
        found = []
        for k in range(4):
            part = terms[k * pitch : (k + 1) * pitch]
            if k < 3:
                part = part + terms[(4 + k) * pitch : (5 + k) * pitch]
            found.append(jnp.sum(jnp.where(here, part, 0.0), axis=0, keepdims=True))
        return found

    x_copies, edge_copies, down_copies = [], [], []
    for index, step in enumerate(STEPS[:2]):
        half = slice(0, HALF) if step[0] < 0 else slice(HALF, OUTER)
        x_copies.append(remote(16 + index, sum_outer.at[:, half, :], outer_got.at[index], step))
        source = flag_x_low if step[0] < 0 else flag_x_high
        x_copies.append(remote(index, source, flag_x_got.at[index], step))
    for index, step in sorted(enumerate(STEPS), key=lambda entry: -entry[1][1]):
        ends = slice(0, 16) if step[1] == 0 else slice(0, 8) if step[1] < 0 else slice(8, 16)
        if step[0] == 0:
            source, target = part_edge.at[:, ends, :], edge_y_got.at[index - 2]
        else:
            source = part_edge.at[0 if step[0] < 0 else 2, ends, :]
            target = edge_x_got.at[index] if step[1] == 0 else edge_d_got.at[index - 4]
        into = down_copies if step[1] < 0 else edge_copies
        into.append(remote(8 + index, source, target, step))
        if step[1] != 0:
            source = flag_y_low if step[1] < 0 else flag_y_high
            target = flag_y_got.at[index - 2] if step[0] == 0 else flag_d_got.at[index - 4]
            into.append(remote(index, source, target, step))

    def start_down():
        for copy in down_copies:
            copy.start()

    def start_late():
        pl.semaphore_wait(late_sem, 3)
        start_down()

    for_blocks(functools.partial(deposit, acc_first, 0, FIRST), block[0])
    for channel in range(4):
        sum_outer[channel] = total(acc_first, FIRST, channel, 0, OUTER)
        edge = total(acc_first, FIRST, channel, EDGE_AT, EDGE)
        for pair in range(3):
            for side in range(2):
                at = side * 8 + channel * 2
                part_edge[pair, at : at + 2, :] = edge[pair * 4 + side * 2 : pair * 4 + side * 2 + 2, :]
    for load in loads[8:]:
        load.wait()
    flag_x_low[0] = axis[0]
    flag_x_low[1] = drop[0]
    flag_x_high[0] = axis[CX - 1]
    flag_x_high[1] = drop[CX - 1]
    for plane in range(CX):
        flag_y_low[plane : plane + 1, :] = axis[plane, 0:1, :]
        flag_y_low[CX + plane : CX + plane + 1, :] = drop[plane, 0:1, :]
        flag_y_high[plane : plane + 1, :] = axis[plane, CY - 1 : CY, :]
        flag_y_high[CX + plane : CX + plane + 1, :] = drop[plane, CY - 1 : CY, :]

    pl.semaphore_wait(barrier, jnp.where(first_in, len(STEPS) - 3, len(STEPS)))
    for copy in edge_copies:
        copy.start()
    pl.when(jnp.logical_not(first_in))(start_down)
    for copy in x_copies:
        copy.start()
    pl.when(last_in)(lambda: greet(late_sem, (1,)))

    for_blocks(functools.partial(deposit, acc_inner, INNER_AT, INNER), block[1])
    for channel in range(4):
        sum_inner[channel] = total(acc_inner, INNER, channel, 0, INNER)

    for tile in range(2):
        lanes = slice(tile * NZ, (tile + 1) * NZ)
        code_inner[0:MID, lanes] = axis[1 + tile, 1 : CY - 1, :]
        drop_inner[0:MID, lanes] = drop[1 + tile, 1 : CY - 1, :]
    fill_table(table_inner, INNER, sum_inner, code_inner, drop_inner)

    def pick_inner(base, size):
        for ref, found in zip(picked, pick(table_inner, INNER, INNER_AT, base, size)):
            ref[:, pl.ds(base, size)] = found

    for_blocks(pick_inner, block[2])

    from_left, from_right = SENT_BY[(1, 0)], SENT_BY[(-1, 0)]
    for copy in x_copies:
        copy.wait_recv()
    for flag, (own, code) in enumerate(((axis, code_outer), (drop, drop_outer))):
        code[0:MID, 0:NZ] = flag_x_got[from_left, flag, 1 : CY - 1, :]
        code[0:MID, NZ:COLS] = own[0, 1 : CY - 1, :]
        code[HALF : HALF + MID, 0:NZ] = own[CX - 1, 1 : CY - 1, :]
        code[HALF : HALF + MID, NZ:COLS] = flag_x_got[from_right, flag, 1 : CY - 1, :]
    both = [
        jnp.concatenate(
            [
                sum_outer[channel, 0:HALF, :] + outer_got[from_left, channel],
                sum_outer[channel, HALF:OUTER, :] + outer_got[from_right, channel],
            ],
            axis=0,
        )
        for channel in range(4)
    ]
    fill_table(table_outer, OUTER, both, code_outer, drop_outer)

    def pick_outer(base, size):
        for ref, found in zip(picked, pick(table_outer, OUTER, 0, base, size)):
            ref[:, pl.ds(base, size)] += found

    for_blocks(pick_outer, block[3])

    pl.when(first_in)(start_late)
    for copy in edge_copies + down_copies:
        copy.wait_recv()
    for pair in range(3):
        for side, end in enumerate((-1, 1)):
            ends = slice(side * 8, side * 8 + 8)
            whole = part_edge[pair, ends, :] + edge_y_got[SENT_BY[(0, -end)] - 2, pair]
            if pair != 1:
                step = 1 if pair == 0 else -1
                whole = whole + edge_x_got[SENT_BY[(step, 0)], ends, :]
                whole = whole + edge_d_got[SENT_BY[(step, -end)] - 4]
            for channel in range(4):
                at = pair * 4 + side * 2
                sum_edge[channel, at : at + 2, :] = whole[2 * channel : 2 * channel + 2]
            for tile in range(2):
                plane = 2 * pair + tile
                lanes = slice(tile * NZ, (tile + 1) * NZ)
                beyond = -1 if plane == 0 else 1 if plane == CX + 1 else 0
                last = CX - 1 if plane == 0 else 0 if plane == CX + 1 else plane - 1
                inside = 0 if side == 0 else CY - 1
                halo = flag_y_got.at[SENT_BY[(0, -end)] - 2]
                if beyond != 0:
                    halo = flag_d_got.at[SENT_BY[(-beyond, -end)] - 4]
                near = pair * 4 + (1 if side == 0 else 2)
                far = pair * 4 + (0 if side == 0 else 3)
                for flag, (own, code) in enumerate(((axis, code_edge), (drop, drop_edge))):
                    if beyond == 0:
                        value = own[last, inside : inside + 1, :]
                    else:
                        value = flag_x_got[SENT_BY[(-beyond, 0)], flag, inside : inside + 1, :]
                    code[near : near + 1, lanes] = value
                    code[far : far + 1, lanes] = halo[flag * CX + last : flag * CX + last + 1, :]
    fill_table(table_edge, EDGE, sum_edge, code_edge, drop_edge)

    cosine, sine = math.cos(ANGLE), math.sin(ANGLE)

    def finish(base, size):
        lanes = pl.ds(base, size)
        for ref, found in zip(picked, pick(table_edge, EDGE, EDGE_AT, base, size)):
            ref[:, lanes] += found
        mean = [picked[k][:, lanes] for k in range(3)]
        code = codes[:, lanes]
        rel = [vel[k][:, lanes] - mean[k] for k in range(3)]
        along_x = code < 1.5
        along_y = (code > 1.5) & (code < 3.5)
        along_z = code > 3.5
        odd = (code == 1.0) | (code == 3.0) | (code == 5.0)
        turn_by = jnp.where(odd, -sine, sine)
        plain = [cosine * r for r in rel]
        cross = [turn_by * r for r in rel]
        new_x = jnp.where(along_x, rel[0], plain[0] + jnp.where(along_y, cross[2], -cross[1]))
        new_y = jnp.where(along_y, rel[1], plain[1] + jnp.where(along_x, -cross[2], cross[0]))
        new_z = jnp.where(along_z, rel[2], plain[2] + jnp.where(along_x, cross[1], -cross[0]))
        living = rows[:, lanes] != NONE
        for k, new in enumerate((new_x, new_y, new_z)):
            outs[k][:, lanes] = jnp.where(living, mean[k] + new, 0.0)

    for_blocks(finish, block[4])

    stores = [
        pltpu.make_async_copy(outs[k], out_hbm.at[k : k + 1, :], load_sem.at[k]) for k in range(3)
    ]
    for store in stores:
        store.start()
    for copy in x_copies + edge_copies + down_copies:
        copy.wait_send()
    for store in stores:
        store.wait()


def body(positions, velocities, counts, grid_shift, axis_index, droplet):
    hbm = pl.BlockSpec(memory_space=pl.ANY)
    slots = positions.shape[1]
    block = BLOCK
    cells = (CX, CY, NZ)
    vmem = pltpu.VMEM
    return pl.pallas_call(
        functools.partial(kernel, block),
        out_shape=jax.ShapeDtypeStruct(velocities.shape, F32),
        in_specs=[hbm] * 6,
        out_specs=hbm,
        scratch_shapes=[
            pltpu.SMEM((1, 1), I32), pltpu.SMEM((3,), I32),
            *[vmem((1, slots), I32)] * 3, *[vmem((1, slots), F32)] * 3, vmem(cells, I32), vmem(cells, I32),
            *[vmem((1, slots), F32)] * 3,
            pltpu.SemaphoreType.DMA((10,)),
            vmem((1, slots), I32), vmem((COLS, slots), BF16), *[vmem((1, slots), F32)] * 4,
            vmem((7 * FIRST, COLS), F32), vmem((7 * INNER, COLS), F32),
            vmem((4, OUTER, COLS), F32), vmem((4, INNER, COLS), F32), vmem((4, EDGE, COLS), F32),
            vmem((3, 16, COLS), F32),
            vmem((7 * OUTER, COLS), BF16), vmem((7 * INNER, COLS), BF16), vmem((7 * EDGE, COLS), BF16),
            vmem((OUTER, COLS), I32), vmem((OUTER, COLS), I32),
            vmem((INNER, COLS), I32), vmem((INNER, COLS), I32),
            vmem((EDGE, COLS), I32), vmem((EDGE, COLS), I32),
            vmem((2, CY, NZ), I32), vmem((2, CY, NZ), I32),
            vmem((2 * CX, NZ), I32), vmem((2 * CX, NZ), I32),
            vmem((2, 2, CY, NZ), I32), vmem((2, 2 * CX, NZ), I32), vmem((4, 2 * CX, NZ), I32),
            vmem((2, 4, HALF, COLS), F32), vmem((2, 16, COLS), F32),
            vmem((2, 3, 8, COLS), F32), vmem((4, 8, COLS), F32),
            pltpu.SemaphoreType.DMA((18,)),
            pltpu.SemaphoreType.DMA((18,)),
            pltpu.SemaphoreType.REGULAR,
        ],
        compiler_params=pltpu.CompilerParams(
            collective_id=0, has_side_effects=True, vmem_limit_bytes=VMEM_MIB << 20
        ),
        name="collision_step",
    )(counts.reshape(1, 1), grid_shift, positions, velocities, axis_index, droplet)


BLOCK = (8192, 8192, 8192, 8192, 8192)
VMEM_MIB = 58


def solution(mesh):
    placed = (
        P(None, ("slab", "cross")),
        P(None, ("slab", "cross")),
        P(("slab", "cross")),
        P(),
        P("slab", "cross", None),
        P("slab", "cross", None),
    )
    return jax.shard_map(
        body, mesh=mesh, in_specs=placed, out_specs=P(None, ("slab", "cross")), check_vma=False
    )
```

```python
import functools
import math

import jax
import jax.numpy as jnp
from jax import lax
from jax.experimental import pallas as pl
from jax.experimental.pallas import tpu as pltpu
from jax.sharding import PartitionSpec as P

QUANT = 8
NFILL = 8
ANGLE = 130.0 * math.pi / 180.0

F32 = jnp.float32
BF16 = jnp.bfloat16
I32 = jnp.int32
MESH = pl.DeviceIdType.MESH

CX, CY, NZ = 4, 32, 128
COLS = 2 * NZ
EDGE, SIDE = 16, 32
HIGH_AT = EDGE
LOW_AT = HIGH_AT + SIDE
INNER_AT = LOW_AT + SIDE
NONE = 127
MID = CY - 2

STEPS = ((-1, 0), (1, 0), (0, -1), (0, 1), (-1, -1), (-1, 1), (1, -1), (1, 1))
SENT_BY = {step: index for index, step in enumerate(STEPS)}


def split(value):
    high = value.astype(BF16)
    low = (value - high.astype(F32)).astype(BF16)
    return high, low


def as_bf16(value):
    return value.astype(F32).astype(BF16)


def kernel(
    block,
    counts_in, shift_in, pos_in, vel_in, axis_in, drop_in, out_hbm,
    counts, shift, pos_x, pos_y, pos_z, vel_x, vel_y, vel_z, axis, drop, out_x, out_y, out_z, load_sem,
    rows, onehots, mean_x, mean_y, mean_z, codes,
    acc_first, acc_second, sum_low, sum_high, sum_inner, sum_edge, part_edge,
    table_low, table_high, table_inner, table_edge,
    code_low, drop_low, code_high, drop_high, code_inner, drop_inner, code_edge, drop_edge,
    flag_x_low, flag_x_high, flag_y_low, flag_y_high,
    flag_x_got, flag_y_got, flag_d_got,
    sums_got, edge_x_got, edge_y_got, edge_d_got,
    send_sem, recv_sem, late_sem,
):
    slots = rows.shape[1]
    vel = (vel_x, vel_y, vel_z)
    outs = (out_x, out_y, out_z)
    picked = (mean_x, mean_y, mean_z, codes)
    slabs, crosses = lax.axis_size("slab"), lax.axis_size("cross")
    me_slab, me_cross = lax.axis_index("slab"), lax.axis_index("cross")

    def place(step):
        return (
            lax.rem(me_slab + step[0] + slabs, slabs),
            lax.rem(me_cross + step[1] + crosses, crosses),
        )

    first_in = me_cross == 0
    last_in = me_cross == crosses - 1

    def greet(semaphore, ends):
        for step in STEPS:
            if step[1] in ends:
                pl.semaphore_signal(semaphore, inc=1, device_id=place(step), device_id_type=MESH)

    barrier = pltpu.get_barrier_semaphore()
    greet(barrier, (-1, 0))
    pl.when(jnp.logical_not(last_in))(lambda: greet(barrier, (1,)))

    loads = [
        pltpu.make_async_copy(source, target, load_sem.at[index])
        for index, (source, target) in enumerate((
            (counts_in, counts), (shift_in, shift),
            (pos_in.at[0:1, :], pos_x), (pos_in.at[1:2, :], pos_y), (pos_in.at[2:3, :], pos_z),
            (vel_in.at[0:1, :], vel_x), (vel_in.at[1:2, :], vel_y), (vel_in.at[2:3, :], vel_z),
            (axis_in, axis), (drop_in, drop),
        ))
    ]
    for load in loads:
        load.start()

    def remote(index, source, target, step):
        return pltpu.make_async_remote_copy(
            src_ref=source,
            dst_ref=target,
            send_sem=send_sem.at[index],
            recv_sem=recv_sem.at[index],
            device_id=place(step),
            device_id_type=MESH,
        )

    def for_blocks(step, size):
        def run(index, carry):
            step(pl.multiple_of(index * size, size), size)
            return carry

        lax.fori_loop(0, slots // size, run, 0)

    acc_first[...] = jnp.zeros_like(acc_first)
    acc_second[...] = jnp.zeros_like(acc_second)
    for ref in (
        code_low, drop_low, code_high, drop_high, code_inner, drop_inner, code_edge, drop_edge, sum_edge
    ):
        ref[...] = jnp.zeros_like(ref)

    anchor_x = me_slab * (CX * QUANT)
    anchor_y = me_cross * (CY * QUANT)
    period_x = slabs * CX * QUANT
    period_y = crosses * CY * QUANT
    for load in loads[:8]:
        load.wait()
    count = counts[0, 0]
    shift_x, shift_y, shift_z = shift[0], shift[1], shift[2]

    def find(base, size):
        lanes = pl.ds(base, size)
        x = (((pos_x[:, lanes] - anchor_x + QUANT) & (period_x - 1)) + shift_x) >> 3
        y = (((pos_y[:, lanes] - anchor_y + QUANT) & (period_y - 1)) + shift_y) >> 3
        z = ((pos_z[:, lanes] + shift_z) >> 3) & (NZ - 1)
        pair = x >> 1
        at_low, at_high = y < 2, y >= CY
        edge = pair * 4 + jnp.where(at_high, -MID, 0)
        other = jnp.where(pair == 1, INNER_AT - 2, jnp.where(pair == 0, LOW_AT - 2, HIGH_AT - 2))
        row = jnp.where(at_low | at_high, edge, other) + y
        living = lax.broadcasted_iota(I32, (1, size), 1) + base < count
        row = jnp.where(living, row, NONE)
        rows[:, lanes] = row
        column = as_bf16((x & 1) * NZ + z)
        ids = as_bf16(lax.broadcasted_iota(I32, (COLS, size), 0))
        onehot = jnp.where(ids == column, jnp.ones((), BF16), jnp.zeros((), BF16))
        onehots[:, lanes] = onehot
        return row, onehot

    def deposit(acc, first, pitch, base, size):
        lanes = pl.ds(base, size)
        if first == 0:
            row, onehot = find(base, size)
        else:
            row, onehot = rows[:, lanes], onehots[:, lanes]
        ids = as_bf16(lax.broadcasted_iota(I32, (pitch, size), 0) + first)
        here = ids == as_bf16(row)
        nought = jnp.zeros((), BF16)
        parts = [jnp.where(here, jnp.ones((1, size), BF16), nought)]
        for k in range(3):
            for term in split(vel[k][:, lanes]):
                parts.append(jnp.where(here, term, nought))
        acc[...] += lax.dot_general(
            jnp.concatenate(parts, axis=0), onehot, (((1,), (1,)), ((), ())),
            preferred_element_type=F32,
        )

    def total(acc, pitch, channel, first, size):
        if channel == 0:
            return acc[first : first + size, :]
        high = (2 * channel - 1) * pitch + first
        low = high + pitch
        return acc[high : high + size, :] + acc[low : low + size, :]

    def fill_table(table, pitch, sums, code, wall):
        number = jnp.maximum(sums[0], jnp.where(wall[...] == 1, float(NFILL), 1.0))
        for k in range(3):
            high, low = split(sums[1 + k] / number)
            table[k * pitch : (k + 1) * pitch, :] = high
            table[(4 + k) * pitch : (5 + k) * pitch, :] = low
        table[3 * pitch : 4 * pitch, :] = as_bf16(code[...])

    def pick(table, pitch, first, base, size):
        lanes = pl.ds(base, size)
        onehot = onehots[:, lanes]
        here = lax.broadcasted_iota(I32, (pitch, size), 0) + first == rows[:, lanes]
        terms = jnp.dot(table[...], onehot, preferred_element_type=F32)
        found = []
        for k in range(4):
            part = terms[k * pitch : (k + 1) * pitch]
            if k < 3:
                part = part + terms[(4 + k) * pitch : (5 + k) * pitch]
            found.append(jnp.sum(jnp.where(here, part, 0.0), axis=0, keepdims=True))
        return found

    to_below = remote(16, sum_low, sums_got.at[0], (-1, 0))
    to_above = remote(17, sum_high, sums_got.at[1], (1, 0))
    flag_copies, edge_copies, down_copies = [], [], []
    for index, step in sorted(enumerate(STEPS), key=lambda entry: (-abs(entry[1][0] * entry[1][1]), -entry[1][1])):
        ends = slice(0, 16) if step[1] == 0 else slice(0, 8) if step[1] < 0 else slice(8, 16)
        if step[0] == 0:
            source, target = part_edge.at[:, ends, :], edge_y_got.at[index - 2]
        else:
            source = part_edge.at[0 if step[0] < 0 else 2, ends, :]
            target = edge_x_got.at[index] if step[1] == 0 else edge_d_got.at[index - 4]
        into = down_copies if step[1] < 0 else edge_copies
        into.append(remote(8 + index, source, target, step))
    for index, step in enumerate(STEPS):
        if step[1] == 0:
            source = flag_x_low if step[0] < 0 else flag_x_high
            flag_copies.append(remote(index, source, flag_x_got.at[index], step))
        else:
            source = flag_y_low if step[1] < 0 else flag_y_high
            target = flag_y_got.at[index - 2] if step[0] == 0 else flag_d_got.at[index - 4]
            into = down_copies if step[1] < 0 else flag_copies
            into.append(remote(index, source, target, step))

    def start_down():
        for copy in down_copies:
            copy.start()

    def start_late():
        pl.semaphore_wait(late_sem, 3)
        start_down()

    first, second = EDGE + SIDE, 2 * SIDE
    for_blocks(functools.partial(deposit, acc_first, 0, first), block[0])
    for channel in range(4):
        sum_high[channel] = total(acc_first, first, channel, HIGH_AT, SIDE)
        edge = total(acc_first, first, channel, 0, EDGE)
        for pair in range(3):
            for side in range(2):
                at = side * 8 + channel * 2
                part_edge[pair, at : at + 2, :] = edge[pair * 4 + side * 2 : pair * 4 + side * 2 + 2, :]
    for load in loads[8:]:
        load.wait()
    flag_x_low[0] = axis[0]
    flag_x_low[1] = drop[0]
    flag_x_high[0] = axis[CX - 1]
    flag_x_high[1] = drop[CX - 1]
    for plane in range(CX):
        flag_y_low[plane : plane + 1, :] = axis[plane, 0:1, :]
        flag_y_low[CX + plane : CX + plane + 1, :] = drop[plane, 0:1, :]
        flag_y_high[plane : plane + 1, :] = axis[plane, CY - 1 : CY, :]
        flag_y_high[CX + plane : CX + plane + 1, :] = drop[plane, CY - 1 : CY, :]

    pl.semaphore_wait(barrier, jnp.where(first_in, len(STEPS) - 3, len(STEPS)))
    for copy in edge_copies:
        copy.start()
    pl.when(jnp.logical_not(first_in))(start_down)
    for copy in flag_copies:
        copy.start()
    to_above.start()
    pl.when(last_in)(lambda: greet(late_sem, (1,)))

    for_blocks(functools.partial(deposit, acc_second, LOW_AT, second), block[1])
    for channel in range(4):
        sum_low[channel] = total(acc_second, second, channel, 0, SIDE)
    to_below.start()
    for channel in range(4):
        sum_inner[channel] = total(acc_second, second, channel, SIDE, SIDE)

    def pick_into(table, at, more, base, size):
        for ref, found in zip(picked, pick(table, SIDE, at, base, size)):
            lanes = pl.ds(base, size)
            ref[:, lanes] = ref[:, lanes] + found if more else found

    for tile in range(2):
        lanes = slice(tile * NZ, (tile + 1) * NZ)
        code_inner[0:MID, lanes] = axis[1 + tile, 1 : CY - 1, :]
        drop_inner[0:MID, lanes] = drop[1 + tile, 1 : CY - 1, :]
    fill_table(table_inner, SIDE, sum_inner, code_inner, drop_inner)
    for_blocks(functools.partial(pick_into, table_inner, INNER_AT, False), block[2])

    from_below, from_above = SENT_BY[(1, 0)], SENT_BY[(-1, 0)]

    def pick_low():
        to_above.wait_recv()
        flag_copies[from_below].wait_recv()
        for flag, (own, code) in enumerate(((axis, code_low), (drop, drop_low))):
            code[0:MID, 0:NZ] = flag_x_got[from_below, flag, 1 : CY - 1, :]
            code[0:MID, NZ:COLS] = own[0, 1 : CY - 1, :]
        both = [sum_low[channel] + sums_got[from_below, channel] for channel in range(4)]
        fill_table(table_low, SIDE, both, code_low, drop_low)
        for_blocks(functools.partial(pick_into, table_low, LOW_AT, True), block[3])

    def pick_high():
        to_below.wait_recv()
        flag_copies[from_above].wait_recv()
        for flag, (own, code) in enumerate(((axis, code_high), (drop, drop_high))):
            code[0:MID, 0:NZ] = own[CX - 1, 1 : CY - 1, :]
            code[0:MID, NZ:COLS] = flag_x_got[from_above, flag, 1 : CY - 1, :]
        both = [sum_high[channel] + sums_got[from_above, channel] for channel in range(4)]
        fill_table(table_high, SIDE, both, code_high, drop_high)
        for_blocks(functools.partial(pick_into, table_high, HIGH_AT, True), block[3])

    second_core = lax.rem(me_slab, 2) == 1
    pl.when(jnp.logical_not(second_core))(pick_high)
    pick_low()
    pl.when(second_core)(pick_high)

    pl.when(first_in)(start_late)
    for copy in edge_copies + flag_copies[2:] + down_copies:
        copy.wait_recv()
    for pair in range(3):
        for side, end in enumerate((-1, 1)):
            ends = slice(side * 8, side * 8 + 8)
            whole = part_edge[pair, ends, :] + edge_y_got[SENT_BY[(0, -end)] - 2, pair]
            if pair != 1:
                step = 1 if pair == 0 else -1
                whole = whole + edge_x_got[SENT_BY[(step, 0)], ends, :]
                whole = whole + edge_d_got[SENT_BY[(step, -end)] - 4]
            for channel in range(4):
                at = pair * 4 + side * 2
                sum_edge[channel, at : at + 2, :] = whole[2 * channel : 2 * channel + 2]
            for tile in range(2):
                plane = 2 * pair + tile
                lanes = slice(tile * NZ, (tile + 1) * NZ)
                beyond = -1 if plane == 0 else 1 if plane == CX + 1 else 0
                last = CX - 1 if plane == 0 else 0 if plane == CX + 1 else plane - 1
                inside = 0 if side == 0 else CY - 1
                halo = flag_y_got.at[SENT_BY[(0, -end)] - 2]
                if beyond != 0:
                    halo = flag_d_got.at[SENT_BY[(-beyond, -end)] - 4]
                near = pair * 4 + (1 if side == 0 else 2)
                far = pair * 4 + (0 if side == 0 else 3)
                for flag, (own, code) in enumerate(((axis, code_edge), (drop, drop_edge))):
                    if beyond == 0:
                        value = own[last, inside : inside + 1, :]
                    else:
                        value = flag_x_got[SENT_BY[(-beyond, 0)], flag, inside : inside + 1, :]
                    code[near : near + 1, lanes] = value
                    code[far : far + 1, lanes] = halo[flag * CX + last : flag * CX + last + 1, :]
    fill_table(table_edge, EDGE, sum_edge, code_edge, drop_edge)

    cosine, sine = math.cos(ANGLE), math.sin(ANGLE)

    def finish(base, size):
        lanes = pl.ds(base, size)
        for ref, found in zip(picked, pick(table_edge, EDGE, 0, base, size)):
            ref[:, lanes] += found
        mean = [picked[k][:, lanes] for k in range(3)]
        code = codes[:, lanes]
        rel = [vel[k][:, lanes] - mean[k] for k in range(3)]
        along_x = code < 1.5
        along_y = (code > 1.5) & (code < 3.5)
        along_z = code > 3.5
        odd = (code == 1.0) | (code == 3.0) | (code == 5.0)
        turn_by = jnp.where(odd, -sine, sine)
        plain = [cosine * r for r in rel]
        cross = [turn_by * r for r in rel]
        new_x = jnp.where(along_x, rel[0], plain[0] + jnp.where(along_y, cross[2], -cross[1]))
        new_y = jnp.where(along_y, rel[1], plain[1] + jnp.where(along_x, -cross[2], cross[0]))
        new_z = jnp.where(along_z, rel[2], plain[2] + jnp.where(along_x, cross[1], -cross[0]))
        living = rows[:, lanes] != NONE
        for k, new in enumerate((new_x, new_y, new_z)):
            outs[k][:, lanes] = jnp.where(living, mean[k] + new, 0.0)

    for_blocks(finish, block[4])

    stores = [
        pltpu.make_async_copy(outs[k], out_hbm.at[k : k + 1, :], load_sem.at[k]) for k in range(3)
    ]
    for store in stores:
        store.start()
    for copy in [to_below, to_above] + edge_copies + flag_copies + down_copies:
        copy.wait_send()
    for store in stores:
        store.wait()


def body(positions, velocities, counts, grid_shift, axis_index, droplet):
    hbm = pl.BlockSpec(memory_space=pl.ANY)
    slots = positions.shape[1]
    block = BLOCK
    cells = (CX, CY, NZ)
    vmem = pltpu.VMEM
    return pl.pallas_call(
        functools.partial(kernel, block),
        out_shape=jax.ShapeDtypeStruct(velocities.shape, F32),
        in_specs=[hbm] * 6,
        out_specs=hbm,
        scratch_shapes=[
            pltpu.SMEM((1, 1), I32), pltpu.SMEM((3,), I32),
            *[vmem((1, slots), I32)] * 3, *[vmem((1, slots), F32)] * 3, vmem(cells, I32), vmem(cells, I32),
            *[vmem((1, slots), F32)] * 3,
            pltpu.SemaphoreType.DMA((10,)),
            vmem((1, slots), I32), vmem((COLS, slots), BF16), *[vmem((1, slots), F32)] * 4,
            vmem((7 * (EDGE + SIDE), COLS), F32), vmem((7 * 2 * SIDE, COLS), F32),
            *[vmem((4, SIDE, COLS), F32)] * 3, vmem((4, EDGE, COLS), F32), vmem((3, 16, COLS), F32),
            *[vmem((7 * SIDE, COLS), BF16)] * 3, vmem((7 * EDGE, COLS), BF16),
            *[vmem((SIDE, COLS), I32)] * 6, *[vmem((EDGE, COLS), I32)] * 2,
            vmem((2, CY, NZ), I32), vmem((2, CY, NZ), I32),
            vmem((2 * CX, NZ), I32), vmem((2 * CX, NZ), I32),
            vmem((2, 2, CY, NZ), I32), vmem((2, 2 * CX, NZ), I32), vmem((4, 2 * CX, NZ), I32),
            vmem((2, 4, SIDE, COLS), F32), vmem((2, 16, COLS), F32),
            vmem((2, 3, 8, COLS), F32), vmem((4, 8, COLS), F32),
            pltpu.SemaphoreType.DMA((18,)),
            pltpu.SemaphoreType.DMA((18,)),
            pltpu.SemaphoreType.REGULAR,
        ],
        compiler_params=pltpu.CompilerParams(
            collective_id=0, has_side_effects=True, vmem_limit_bytes=VMEM_MIB << 20
        ),
        name="collision_step",
    )(counts.reshape(1, 1), grid_shift, positions, velocities, axis_index, droplet)


BLOCK = (8192, 8192, 16384, 16384, 16384)
VMEM_MIB = 58


def solution(mesh):
    placed = (
        P(None, ("slab", "cross")),
        P(None, ("slab", "cross")),
        P(("slab", "cross")),
        P(),
        P("slab", "cross", None),
        P("slab", "cross", None),
    )
    return jax.shard_map(
        body, mesh=mesh, in_specs=placed, out_specs=P(None, ("slab", "cross")), check_vma=False
    )
```

```python
import functools
import math

import jax
import jax.numpy as jnp
from jax import lax
from jax.experimental import pallas as pl
from jax.experimental.pallas import tpu as pltpu
from jax.sharding import PartitionSpec as P

QUANT = 8
NFILL = 8
ANGLE = 130.0 * math.pi / 180.0

F32 = jnp.float32
BF16 = jnp.bfloat16
I32 = jnp.int32
MESH = pl.DeviceIdType.MESH

CX, CY, NZ = 4, 32, 128
COLS = 2 * NZ
EDGE, SIDE = 16, 32
HIGH_AT = EDGE
LOW_AT = HIGH_AT + SIDE
INNER_AT = LOW_AT + SIDE
NONE = 127
MID = CY - 2

STEPS = ((-1, 0), (1, 0), (0, -1), (0, 1), (-1, -1), (-1, 1), (1, -1), (1, 1))
SENT_BY = {step: index for index, step in enumerate(STEPS)}


def split(value):
    high = value.astype(BF16)
    low = (value - high.astype(F32)).astype(BF16)
    return high, low


def as_bf16(value):
    return value.astype(F32).astype(BF16)


def kernel(
    block,
    counts_in, shift_in, pos_in, vel_in, axis_in, drop_in, out_hbm,
    counts, shift, pos_x, pos_y, pos_z, vel_x, vel_y, vel_z, axis, drop, out_x, out_y, out_z, load_sem,
    rows, onehots, mean_x, mean_y, mean_z, codes,
    acc_first, acc_second, sum_low, sum_high, sum_inner, sum_edge, part_edge,
    table_low, table_high, table_inner, table_edge,
    code_low, drop_low, code_high, drop_high, code_inner, drop_inner, code_edge, drop_edge,
    flag_x_low, flag_x_high, flag_y_low, flag_y_high,
    flag_x_got, flag_y_got, flag_d_got,
    sums_got, edge_x_got, edge_y_got, edge_d_got,
    send_sem, recv_sem, late_sem, row_sem,
):
    slots = rows.shape[1]
    vel = (vel_x, vel_y, vel_z)
    outs = (out_x, out_y, out_z)
    picked = (mean_x, mean_y, mean_z, codes)
    slabs, crosses = lax.axis_size("slab"), lax.axis_size("cross")
    me_slab, me_cross = lax.axis_index("slab"), lax.axis_index("cross")

    def place(step):
        return (
            lax.rem(me_slab + step[0] + slabs, slabs),
            lax.rem(me_cross + step[1] + crosses, crosses),
        )

    first_in = me_cross == 0
    last_in = me_cross == crosses - 1

    def greet(semaphore, ends):
        for step in STEPS:
            if step[1] in ends:
                pl.semaphore_signal(semaphore, inc=1, device_id=place(step), device_id_type=MESH)

    barrier = pltpu.get_barrier_semaphore()
    greet(barrier, (-1, 0))
    pl.when(jnp.logical_not(last_in))(lambda: greet(barrier, (1,)))

    loads = [
        pltpu.make_async_copy(source, target, load_sem.at[index])
        for index, (source, target) in enumerate((
            (counts_in, counts), (shift_in, shift), (axis_in, axis), (drop_in, drop),
        ))
    ]

    def load_rows(base, size):
        lanes = pl.ds(base, size)
        return [
            pltpu.make_async_copy(
                source.at[k : k + 1, lanes], target.at[:, lanes], row_sem.at[base // size, at + k]
            )
            for at, source, targets in ((0, pos_in, (pos_x, pos_y, pos_z)), (3, vel_in, vel))
            for k, target in enumerate(targets)
        ]

    for load in loads[:2]:
        load.start()
    for base in range(0, slots, block[0]):
        for load in load_rows(base, block[0]):
            load.start()
    for load in loads[2:]:
        load.start()

    def remote(index, source, target, step):
        return pltpu.make_async_remote_copy(
            src_ref=source,
            dst_ref=target,
            send_sem=send_sem.at[index],
            recv_sem=recv_sem.at[index],
            device_id=place(step),
            device_id_type=MESH,
        )

    def for_blocks(step, size):
        def run(index, carry):
            step(pl.multiple_of(index * size, size), size)
            return carry

        lax.fori_loop(0, slots // size, run, 0)

    acc_first[...] = jnp.zeros_like(acc_first)
    acc_second[...] = jnp.zeros_like(acc_second)
    for ref in (
        code_low, drop_low, code_high, drop_high, code_inner, drop_inner, code_edge, drop_edge, sum_edge
    ):
        ref[...] = jnp.zeros_like(ref)

    anchor_x = me_slab * (CX * QUANT)
    anchor_y = me_cross * (CY * QUANT)
    period_x = slabs * CX * QUANT
    period_y = crosses * CY * QUANT
    for load in loads[:2]:
        load.wait()
    count = counts[0, 0]
    shift_x, shift_y, shift_z = shift[0], shift[1], shift[2]

    def find(base, size):
        lanes = pl.ds(base, size)
        for load in load_rows(base, size):
            load.wait()
        x = (((pos_x[:, lanes] - anchor_x + QUANT) & (period_x - 1)) + shift_x) >> 3
        y = (((pos_y[:, lanes] - anchor_y + QUANT) & (period_y - 1)) + shift_y) >> 3
        z = ((pos_z[:, lanes] + shift_z) >> 3) & (NZ - 1)
        pair = x >> 1
        at_low, at_high = y < 2, y >= CY
        edge = pair * 4 + jnp.where(at_high, -MID, 0)
        other = jnp.where(pair == 1, INNER_AT - 2, jnp.where(pair == 0, LOW_AT - 2, HIGH_AT - 2))
        row = jnp.where(at_low | at_high, edge, other) + y
        living = lax.broadcasted_iota(I32, (1, size), 1) + base < count
        row = jnp.where(living, row, NONE)
        rows[:, lanes] = row
        column = as_bf16((x & 1) * NZ + z)
        ids = as_bf16(lax.broadcasted_iota(I32, (COLS, size), 0))
        onehot = jnp.where(ids == column, jnp.ones((), BF16), jnp.zeros((), BF16))
        onehots[:, lanes] = onehot
        return row, onehot

    def deposit(acc, first, pitch, base, size):
        lanes = pl.ds(base, size)
        if first == 0:
            row, onehot = find(base, size)
        else:
            row, onehot = rows[:, lanes], onehots[:, lanes]
        ids = as_bf16(lax.broadcasted_iota(I32, (pitch, size), 0) + first)
        here = ids == as_bf16(row)
        nought = jnp.zeros((), BF16)
        parts = [jnp.where(here, jnp.ones((1, size), BF16), nought)]
        for k in range(3):
            for term in split(vel[k][:, lanes]):
                parts.append(jnp.where(here, term, nought))
        acc[...] += lax.dot_general(
            jnp.concatenate(parts, axis=0), onehot, (((1,), (1,)), ((), ())),
            preferred_element_type=F32,
        )

    def total(acc, pitch, channel, first, size):
        if channel == 0:
            return acc[first : first + size, :]
        high = (2 * channel - 1) * pitch + first
        low = high + pitch
        return acc[high : high + size, :] + acc[low : low + size, :]

    def fill_table(table, pitch, sums, code, wall):
        number = jnp.maximum(sums[0], jnp.where(wall[...] == 1, float(NFILL), 1.0))
        for k in range(3):
            high, low = split(sums[1 + k] / number)
            table[k * pitch : (k + 1) * pitch, :] = high
            table[(4 + k) * pitch : (5 + k) * pitch, :] = low
        table[3 * pitch : 4 * pitch, :] = as_bf16(code[...])

    def pick(table, pitch, first, base, size):
        lanes = pl.ds(base, size)
        onehot = onehots[:, lanes]
        here = lax.broadcasted_iota(I32, (pitch, size), 0) + first == rows[:, lanes]
        terms = jnp.dot(table[...], onehot, preferred_element_type=F32)
        found = []
        for k in range(4):
            part = terms[k * pitch : (k + 1) * pitch]
            if k < 3:
                part = part + terms[(4 + k) * pitch : (5 + k) * pitch]
            found.append(jnp.sum(jnp.where(here, part, 0.0), axis=0, keepdims=True))
        return found

    to_below = remote(16, sum_low, sums_got.at[0], (-1, 0))
    to_above = remote(17, sum_high, sums_got.at[1], (1, 0))
    flag_copies, edge_copies, down_copies = [], [], []
    for index, step in sorted(enumerate(STEPS), key=lambda entry: (-abs(entry[1][0] * entry[1][1]), -entry[1][1])):
        ends = slice(0, 16) if step[1] == 0 else slice(0, 8) if step[1] < 0 else slice(8, 16)
        if step[0] == 0:
            source, target = part_edge.at[:, ends, :], edge_y_got.at[index - 2]
        else:
            source = part_edge.at[0 if step[0] < 0 else 2, ends, :]
            target = edge_x_got.at[index] if step[1] == 0 else edge_d_got.at[index - 4]
        into = down_copies if step[1] < 0 else edge_copies
        into.append(remote(8 + index, source, target, step))
    for index, step in enumerate(STEPS):
        if step[1] == 0:
            source = flag_x_low if step[0] < 0 else flag_x_high
            flag_copies.append(remote(index, source, flag_x_got.at[index], step))
        else:
            source = flag_y_low if step[1] < 0 else flag_y_high
            target = flag_y_got.at[index - 2] if step[0] == 0 else flag_d_got.at[index - 4]
            into = down_copies if step[1] < 0 else flag_copies
            into.append(remote(index, source, target, step))

    def start_down():
        for copy in down_copies:
            copy.start()

    def start_late():
        pl.semaphore_wait(late_sem, 3)
        start_down()

    first, second = EDGE + SIDE, 2 * SIDE
    for_blocks(functools.partial(deposit, acc_first, 0, first), block[0])
    for channel in range(4):
        sum_high[channel] = total(acc_first, first, channel, HIGH_AT, SIDE)
        edge = total(acc_first, first, channel, 0, EDGE)
        for pair in range(3):
            for side in range(2):
                at = side * 8 + channel * 2
                part_edge[pair, at : at + 2, :] = edge[pair * 4 + side * 2 : pair * 4 + side * 2 + 2, :]
    for load in loads[2:]:
        load.wait()
    flag_x_low[0] = axis[0]
    flag_x_low[1] = drop[0]
    flag_x_high[0] = axis[CX - 1]
    flag_x_high[1] = drop[CX - 1]
    for plane in range(CX):
        flag_y_low[plane : plane + 1, :] = axis[plane, 0:1, :]
        flag_y_low[CX + plane : CX + plane + 1, :] = drop[plane, 0:1, :]
        flag_y_high[plane : plane + 1, :] = axis[plane, CY - 1 : CY, :]
        flag_y_high[CX + plane : CX + plane + 1, :] = drop[plane, CY - 1 : CY, :]

    pl.semaphore_wait(barrier, jnp.where(first_in, len(STEPS) - 3, len(STEPS)))
    for copy in edge_copies:
        copy.start()
    pl.when(jnp.logical_not(first_in))(start_down)
    for copy in flag_copies:
        copy.start()
    to_above.start()
    pl.when(last_in)(lambda: greet(late_sem, (1,)))

    for_blocks(functools.partial(deposit, acc_second, LOW_AT, second), block[1])
    for channel in range(4):
        sum_low[channel] = total(acc_second, second, channel, 0, SIDE)
    to_below.start()
    for channel in range(4):
        sum_inner[channel] = total(acc_second, second, channel, SIDE, SIDE)

    def pick_into(table, at, more, base, size):
        for ref, found in zip(picked, pick(table, SIDE, at, base, size)):
            lanes = pl.ds(base, size)
            ref[:, lanes] = ref[:, lanes] + found if more else found

    for tile in range(2):
        lanes = slice(tile * NZ, (tile + 1) * NZ)
        code_inner[0:MID, lanes] = axis[1 + tile, 1 : CY - 1, :]
        drop_inner[0:MID, lanes] = drop[1 + tile, 1 : CY - 1, :]
    fill_table(table_inner, SIDE, sum_inner, code_inner, drop_inner)
    for_blocks(functools.partial(pick_into, table_inner, INNER_AT, False), block[2])

    from_below, from_above = SENT_BY[(1, 0)], SENT_BY[(-1, 0)]

    def pick_low():
        to_above.wait_recv()
        flag_copies[from_below].wait_recv()
        for flag, (own, code) in enumerate(((axis, code_low), (drop, drop_low))):
            code[0:MID, 0:NZ] = flag_x_got[from_below, flag, 1 : CY - 1, :]
            code[0:MID, NZ:COLS] = own[0, 1 : CY - 1, :]
        both = [sum_low[channel] + sums_got[from_below, channel] for channel in range(4)]
        fill_table(table_low, SIDE, both, code_low, drop_low)
        for_blocks(functools.partial(pick_into, table_low, LOW_AT, True), block[3])

    def pick_high():
        to_below.wait_recv()
        flag_copies[from_above].wait_recv()
        for flag, (own, code) in enumerate(((axis, code_high), (drop, drop_high))):
            code[0:MID, 0:NZ] = own[CX - 1, 1 : CY - 1, :]
            code[0:MID, NZ:COLS] = flag_x_got[from_above, flag, 1 : CY - 1, :]
        both = [sum_high[channel] + sums_got[from_above, channel] for channel in range(4)]
        fill_table(table_high, SIDE, both, code_high, drop_high)
        for_blocks(functools.partial(pick_into, table_high, HIGH_AT, True), block[3])

    second_core = lax.rem(me_slab, 2) == 1
    pl.when(jnp.logical_not(second_core))(pick_high)
    pick_low()
    pl.when(second_core)(pick_high)

    pl.when(first_in)(start_late)
    for copy in edge_copies + flag_copies[2:] + down_copies:
        copy.wait_recv()
    for pair in range(3):
        for side, end in enumerate((-1, 1)):
            ends = slice(side * 8, side * 8 + 8)
            whole = part_edge[pair, ends, :] + edge_y_got[SENT_BY[(0, -end)] - 2, pair]
            if pair != 1:
                step = 1 if pair == 0 else -1
                whole = whole + edge_x_got[SENT_BY[(step, 0)], ends, :]
                whole = whole + edge_d_got[SENT_BY[(step, -end)] - 4]
            for channel in range(4):
                at = pair * 4 + side * 2
                sum_edge[channel, at : at + 2, :] = whole[2 * channel : 2 * channel + 2]
            for tile in range(2):
                plane = 2 * pair + tile
                lanes = slice(tile * NZ, (tile + 1) * NZ)
                beyond = -1 if plane == 0 else 1 if plane == CX + 1 else 0
                last = CX - 1 if plane == 0 else 0 if plane == CX + 1 else plane - 1
                inside = 0 if side == 0 else CY - 1
                halo = flag_y_got.at[SENT_BY[(0, -end)] - 2]
                if beyond != 0:
                    halo = flag_d_got.at[SENT_BY[(-beyond, -end)] - 4]
                near = pair * 4 + (1 if side == 0 else 2)
                far = pair * 4 + (0 if side == 0 else 3)
                for flag, (own, code) in enumerate(((axis, code_edge), (drop, drop_edge))):
                    if beyond == 0:
                        value = own[last, inside : inside + 1, :]
                    else:
                        value = flag_x_got[SENT_BY[(-beyond, 0)], flag, inside : inside + 1, :]
                    code[near : near + 1, lanes] = value
                    code[far : far + 1, lanes] = halo[flag * CX + last : flag * CX + last + 1, :]
    fill_table(table_edge, EDGE, sum_edge, code_edge, drop_edge)

    cosine, sine = math.cos(ANGLE), math.sin(ANGLE)

    def finish(base, size):
        lanes = pl.ds(base, size)
        for ref, found in zip(picked, pick(table_edge, EDGE, 0, base, size)):
            ref[:, lanes] += found
        mean = [picked[k][:, lanes] for k in range(3)]
        code = codes[:, lanes]
        rel = [vel[k][:, lanes] - mean[k] for k in range(3)]
        along_x = code < 1.5
        along_y = (code > 1.5) & (code < 3.5)
        along_z = code > 3.5
        odd = (code == 1.0) | (code == 3.0) | (code == 5.0)
        turn_by = jnp.where(odd, -sine, sine)
        plain = [cosine * r for r in rel]
        cross = [turn_by * r for r in rel]
        new_x = jnp.where(along_x, rel[0], plain[0] + jnp.where(along_y, cross[2], -cross[1]))
        new_y = jnp.where(along_y, rel[1], plain[1] + jnp.where(along_x, -cross[2], cross[0]))
        new_z = jnp.where(along_z, rel[2], plain[2] + jnp.where(along_x, cross[1], -cross[0]))
        living = rows[:, lanes] != NONE
        for k, new in enumerate((new_x, new_y, new_z)):
            outs[k][:, lanes] = jnp.where(living, mean[k] + new, 0.0)

    for_blocks(finish, block[4])

    stores = [
        pltpu.make_async_copy(outs[k], out_hbm.at[k : k + 1, :], load_sem.at[k]) for k in range(3)
    ]
    for store in stores:
        store.start()
    for copy in [to_below, to_above] + edge_copies + flag_copies + down_copies:
        copy.wait_send()
    for store in stores:
        store.wait()


def body(positions, velocities, counts, grid_shift, axis_index, droplet):
    hbm = pl.BlockSpec(memory_space=pl.ANY)
    slots = positions.shape[1]
    block = BLOCK
    cells = (CX, CY, NZ)
    vmem = pltpu.VMEM
    return pl.pallas_call(
        functools.partial(kernel, block),
        out_shape=jax.ShapeDtypeStruct(velocities.shape, F32),
        in_specs=[hbm] * 6,
        out_specs=hbm,
        scratch_shapes=[
            pltpu.SMEM((1, 1), I32), pltpu.SMEM((3,), I32),
            *[vmem((1, slots), I32)] * 3, *[vmem((1, slots), F32)] * 3, vmem(cells, I32), vmem(cells, I32),
            *[vmem((1, slots), F32)] * 3,
            pltpu.SemaphoreType.DMA((10,)),
            vmem((1, slots), I32), vmem((COLS, slots), BF16), *[vmem((1, slots), F32)] * 4,
            vmem((7 * (EDGE + SIDE), COLS), F32), vmem((7 * 2 * SIDE, COLS), F32),
            *[vmem((4, SIDE, COLS), F32)] * 3, vmem((4, EDGE, COLS), F32), vmem((3, 16, COLS), F32),
            *[vmem((7 * SIDE, COLS), BF16)] * 3, vmem((7 * EDGE, COLS), BF16),
            *[vmem((SIDE, COLS), I32)] * 6, *[vmem((EDGE, COLS), I32)] * 2,
            vmem((2, CY, NZ), I32), vmem((2, CY, NZ), I32),
            vmem((2 * CX, NZ), I32), vmem((2 * CX, NZ), I32),
            vmem((2, 2, CY, NZ), I32), vmem((2, 2 * CX, NZ), I32), vmem((4, 2 * CX, NZ), I32),
            vmem((2, 4, SIDE, COLS), F32), vmem((2, 16, COLS), F32),
            vmem((2, 3, 8, COLS), F32), vmem((4, 8, COLS), F32),
            pltpu.SemaphoreType.DMA((18,)),
            pltpu.SemaphoreType.DMA((18,)),
            pltpu.SemaphoreType.REGULAR,
            pltpu.SemaphoreType.DMA((slots // block[0], 6)),
        ],
        compiler_params=pltpu.CompilerParams(
            collective_id=0, has_side_effects=True, vmem_limit_bytes=VMEM_MIB << 20
        ),
        name="collision_step",
    )(counts.reshape(1, 1), grid_shift, positions, velocities, axis_index, droplet)


BLOCK = (8192, 8192, 16384, 16384, 16384)
VMEM_MIB = 58


def solution(mesh):
    placed = (
        P(None, ("slab", "cross")),
        P(None, ("slab", "cross")),
        P(("slab", "cross")),
        P(),
        P("slab", "cross", None),
        P("slab", "cross", None),
    )
    return jax.shard_map(
        body, mesh=mesh, in_specs=placed, out_specs=P(None, ("slab", "cross")), check_vma=False
    )
```
